32 devices in a mesh: row: 4 (over x, core), col: 8 (over z, y).
Axes of the slice: x: 2, y: 2, z: 4, core: 2. Of those that a mesh axis runs over, the one named last changes fastest.
Arguments:
- slices: float32 [8, 8192, 8192], P(None, 'row', 'col'), may hold values from -6 to 6
- basis: float32 [8192, 128], P('col'), may hold values from -0.0625 to 0.0625
Outputs:
- gram: float32 [8192, 8192], P('row', 'col')
The draws below stay inside these ranges and needn't reach their ends.
All inputs are finite; a program needn't handle non-finite values.
Results may differ from the reference program's by a relative error of at most 0.0001.
Values sent between devices are 32-bit elements; how exact they have to be, the bound alone decides.
A program may use at most 192 MiB of HBM per device.

```python
import jax
import jax.numpy as jnp
from jax import lax

N = 8192
R = 128
K_WIN = 8


def block_scale(stream_key, dims, pieces, smallest, largest):
    gain = 1.0
    for axis_at, parts in pieces:
        heights = jax.random.uniform(jax.random.fold_in(jax.random.fold_in(stream_key, 6), axis_at), (parts,), jnp.float32, smallest / len(pieces), largest / len(pieces))
        gain = gain * jnp.repeat(jnp.exp(heights), dims[axis_at] // parts).reshape((-1,) + (1,) * (len(dims) - 1 - axis_at))
    return gain


def gaussian(stream_key, extent, deviation, limit, split=(), held_as=jnp.bfloat16):
    result = deviation * jax.random.normal(stream_key, extent, jnp.float32)
    if split:
        result = result * block_scale(stream_key, extent, split, -0.22, 0.18)
    return jnp.clip(result, -limit, limit).astype(held_as)


def setup_inputs(seed: int = 0) -> dict:
    streams_of = jax.random.split(jax.random.key(seed), 3)
    slices = gaussian(streams_of[0], (K_WIN, N, N), 1.0, 6.0, ((1, 4), (2, 8)), jnp.float32)
    basis = gaussian(streams_of[1], (N, R), N ** -0.5, 0.0625, ((0, 8),), jnp.float32)
    return {"slices": slices, "basis": basis}


def reference(slices, basis):
    scale = 1.0 / jnp.sqrt(jnp.float32(K_WIN * R))

    def accumulate(total, one_slice):
        projected = jnp.dot(one_slice, basis, precision=lax.Precision.HIGHEST, preferred_element_type=jnp.float32)
        outer = jnp.dot(projected, projected.T, precision=lax.Precision.HIGHEST, preferred_element_type=jnp.float32)
        return (total + outer, None)
    total, unused = lax.scan(accumulate, jnp.zeros((N, N), jnp.float32), slices)
    return total * scale
```

```python
import functools

import jax
import jax.numpy as jnp
from jax import lax
from jax.experimental import pallas as pl
from jax.experimental.pallas import tpu as pltpu
from jax.sharding import PartitionSpec as P

MESH = pl.DeviceIdType.MESH
QUARTERS = 4
LINE = 4
LAG_REDUCE, LAG_ROOT, LAG_SPREAD, LAG_DONE = 2, 4, 6, 8


def split(value):
    high = value.astype(jnp.bfloat16)
    low = (value - high.astype(jnp.float32)).astype(jnp.bfloat16)
    return high, low


def gram_kernel(
    scale, slices, basis, out,
    part, fin, y_in, za_in, zb_in, yb_in, slab, stream, factor, slab_t, acc,
    stream_sem, y_s, y_r, za_s, za_r, zb_s, zb_r, yb_s, yb_r,
    ca_s, ca_r, cb_s, cb_r, yg_s, yg_r, sa_s, sa_r, sb_s, sb_r, out_sem,
):
    count, rows, depth = slices.shape
    rank = basis.shape[1]
    pairs = count // 2
    segments = pairs * QUARTERS
    half = rows // 2
    a_rows = half // QUARTERS
    b_rows = rows // QUARTERS
    row = lax.axis_index("row")
    col = lax.axis_index("col")
    z, y = col // 2, col % 2
    mate = {"col": z * 2 + 1 - y}
    others = [{"row": lax.rem(row + i, 4)} for i in (1, 2, 3)]
    owner = row == z
    inner = (z > 0) & (z < LINE - 1)

    def at_z(position):
        return {"col": position * 2 + y}

    def place(s):
        return s // QUARTERS, s % QUARTERS

    def root_of(s):
        return LINE // 2 - 1 + s % 2

    def a_part(s, side):
        p, q = place(s)
        return p, pl.ds(pl.multiple_of(side * half + q * a_rows, a_rows), a_rows)

    def b_part(s):
        p, q = place(s)
        return pairs + p, pl.ds(pl.multiple_of(q * b_rows, b_rows), b_rows)

    def remote(src, dst, send, recv, device):
        return pltpu.make_async_remote_copy(
            src_ref=src, dst_ref=dst, send_sem=send, recv_sem=recv,
            device_id=device, device_id_type=MESH,
        )

    def stream_copies(s):
        slot = s % 2
        k, first = a_part(s, 0)
        _, second = a_part(s, 1)
        kb, all_b = b_part(s)
        return [
            pltpu.make_async_copy(slices.at[k, first], stream.at[slot, pl.ds(0, a_rows)], stream_sem.at[slot, 0]),
            pltpu.make_async_copy(slices.at[k, second], stream.at[slot, pl.ds(a_rows, a_rows)], stream_sem.at[slot, 1]),
            pltpu.make_async_copy(slices.at[kb, all_b], stream.at[slot, pl.ds(2 * a_rows, b_rows)], stream_sem.at[slot, 2]),
        ]

    def y_copy(s):
        k, there = a_part(s, 1 - y)
        return remote(part.at[k, there], y_in.at[s], y_s.at[s], y_r.at[s], mate)

    def z_copies(s):
        root = root_of(s)
        target = at_z(jnp.where(z < root, z + 1, jnp.maximum(z - 1, 0)))
        slot = jnp.where(z - 1 == root, segments + s // 2, s)
        k, mine = a_part(s, y)
        kb, all_b = b_part(s)
        return [
            remote(part.at[k, mine], za_in.at[slot], za_s.at[s], za_r.at[slot], target),
            remote(part.at[kb, all_b], zb_in.at[slot], zb_s.at[s], zb_r.at[slot], target),
        ]

    def yb_copy(s):
        kb, all_b = b_part(s)
        return remote(part.at[kb, all_b], yb_in.at[s // 2], yb_s.at[s // 2], yb_r.at[s // 2], mate)

    def a_spread(s, way, to):
        k, mine = a_part(s, y)
        return remote(fin.at[k, mine], fin.at[k, mine], ca_s.at[s, way], ca_r.at[s], at_z(to))

    def b_spread(s, way, to):
        kb, all_b = b_part(s)
        return remote(fin.at[kb, all_b], fin.at[kb, all_b], cb_s.at[s, way], cb_r.at[s], at_z(to))

    def y_gather(s, side):
        k, mine = a_part(s, side)
        return remote(fin.at[k, mine], fin.at[k, mine], yg_s.at[s], yg_r.at[s], mate)

    def slab_a(s):
        k, mine = a_part(s, y)
        _, q = place(s)
        return fin.at[k, mine], slab.at[k, pl.ds(pl.multiple_of(q * a_rows, a_rows), a_rows)]

    def slab_b(s):
        kb, all_b = b_part(s)
        _, q = place(s)
        return fin.at[kb, all_b], slab.at[kb, pl.ds(pl.multiple_of((q % 2) * b_rows, b_rows), b_rows)]

    def in_slab(s):
        return (s % QUARTERS) // 2 == y

    for copy in stream_copies(0):
        copy.start()

    high, low = split(basis[...])
    factor[:, :rank] = high
    factor[:, rank:] = low

    barrier = pltpu.get_barrier_semaphore()
    pl.semaphore_signal(barrier, inc=1, device_id=mate, device_id_type=MESH)
    for device in others:
        pl.semaphore_signal(barrier, inc=1, device_id=device, device_id_type=MESH)

    @pl.when(z > 0)
    def _():
        pl.semaphore_signal(barrier, inc=1, device_id=at_z(jnp.maximum(z - 1, 0)), device_id_type=MESH)

    @pl.when(z < LINE - 1)
    def _():
        pl.semaphore_signal(barrier, inc=1, device_id=at_z(jnp.minimum(z + 1, LINE - 1)), device_id_type=MESH)

    pl.semaphore_wait(barrier, jnp.where(inner, 6, 5))
    acc[...] = jnp.zeros_like(acc)

    def project(s):
        slot = s % 2

        @pl.when(s + 1 < segments)
        def _():
            for copy in stream_copies(s + 1):
                copy.start()

        for copy in stream_copies(s):
            copy.wait()
        p, q = place(s)
        for i in range(4):
            high, low = split(stream[slot, i * a_rows:(i + 1) * a_rows, :])
            both = jnp.dot(high, factor[...], preferred_element_type=jnp.float32)
            both += jnp.dot(low, factor[...], preferred_element_type=jnp.float32)
            value = both[:, :rank] + both[:, rank:]
            if i < 2:
                k, there = a_part(s, i)
            else:
                k = pairs + p
                there = pl.ds(pl.multiple_of(q * b_rows + (i - 2) * a_rows, a_rows), a_rows)
            part[k, there, :] = value
        y_copy(s).start()

    def reduce(s):
        root = root_of(s)
        k, mine = a_part(s, y)
        kb, all_b = b_part(s)
        y_copy(s).wait_recv()
        part[k, mine, :] += y_in[s]

        @pl.when(inner)
        def _():
            pltpu.make_async_copy(za_in.at[s], za_in.at[s], za_r.at[s]).wait()
            part[k, mine, :] += za_in[s]
            pltpu.make_async_copy(zb_in.at[s], zb_in.at[s], zb_r.at[s]).wait()
            part[kb, all_b, :] += zb_in[s]

        @pl.when(z != root)
        def _():
            for copy in z_copies(s):
                copy.start()

        @pl.when(z == root)
        def _():
            second = segments + s // 2
            pltpu.make_async_copy(za_in.at[second], za_in.at[second], za_r.at[second]).wait()
            fin[k, mine, :] = part[k, mine, :] + za_in[second]
            a_spread(s, 0, z - 1).start()
            a_spread(s, 1, z + 1).start()
            y_gather(s, y).start()
            pltpu.make_async_copy(zb_in.at[second], zb_in.at[second], zb_r.at[second]).wait()
            part[kb, all_b, :] += zb_in[second]
            yb_copy(s).start()

    def finish_root(s):
        kb, all_b = b_part(s)

        @pl.when(z == root_of(s))
        def _():
            yb_copy(s).wait_recv()
            fin[kb, all_b, :] = part[kb, all_b, :] + yb_in[s // 2]
            b_spread(s, 0, z - 1).start()
            b_spread(s, 1, z + 1).start()

    def spread(s):
        root = root_of(s)
        outer = jnp.clip(jnp.where(z < root, z - 1, z + 1), 0, LINE - 1)

        @pl.when(z != root)
        def _():
            a_spread(s, 0, outer).wait_recv()

            @pl.when(inner)
            def _():
                a_spread(s, 0, outer).start()

            y_gather(s, y).start()

        @pl.when(z != root)
        def _():
            b_spread(s, 0, outer).wait_recv()

            @pl.when(inner)
            def _():
                b_spread(s, 0, outer).start()

        @pl.when(owner)
        def _():
            src, dst = slab_a(s)
            for i, device in enumerate(others):
                remote(src, dst, sa_s.at[s, i], sa_r.at[s], device).start()
            pltpu.make_async_copy(src, dst, sa_r.at[s]).start()

        @pl.when(owner & in_slab(s))
        def _():
            src, dst = slab_b(s)
            for i, device in enumerate(others):
                remote(src, dst, sb_s.at[s, i], sb_r.at[s], device).start()
            pltpu.make_async_copy(src, dst, sb_r.at[s]).start()

    def done(s):
        y_gather(s, 1 - y).wait_recv()
        src, dst = slab_a(s)
        pltpu.make_async_copy(src, dst, sa_r.at[s]).wait()

        @pl.when(in_slab(s))
        def _():
            src, dst = slab_b(s)
            pltpu.make_async_copy(src, dst, sb_r.at[s]).wait()

    def out_copy(j):
        here = pl.ds(pl.multiple_of(j * b_rows, b_rows), b_rows)
        return pltpu.make_async_copy(acc.at[here], out.at[here], out_sem.at[j])

    def multiply(s):
        p, j = place(s)

        @pl.when(j == 0)
        def _():
            for i, k in enumerate((p, pairs + p)):
                high, low = split((slab[k] * scale).T)
                slab_t[i * rank:(i + 1) * rank, :] = high
                slab_t[(2 + i) * rank:(3 + i) * rank, :] = high
                slab_t[(4 + i) * rank:(5 + i) * rank, :] = low

        for i in range(2):
            here = pl.ds(pl.multiple_of(j * b_rows + i * a_rows, a_rows), a_rows)
            high, low = split(jnp.concatenate([fin[p, here, :], fin[pairs + p, here, :]], axis=1))
            left = jnp.concatenate([high, low, high], axis=1)
            acc[here, :] += jnp.dot(left, slab_t[...], preferred_element_type=jnp.float32)

        @pl.when(p == pairs - 1)
        def _():
            out_copy(j).start()

    def stage(action, s):
        pl.when((s >= 0) & (s < segments))(lambda: action(s))

    def body(t, carry):
        stage(spread, t - LAG_SPREAD)
        stage(finish_root, t - LAG_ROOT)
        stage(reduce, t - LAG_REDUCE)
        stage(project, t)
        stage(done, t - LAG_DONE)
        stage(multiply, t - LAG_DONE - QUARTERS + 1)
        return carry

    lax.fori_loop(0, segments + LAG_DONE + QUARTERS - 1, body, 0)

    def drain(s, carry):
        root = root_of(s)
        y_copy(s).wait_send()
        y_gather(s, y).wait_send()

        @pl.when(z != root)
        def _():
            for copy in z_copies(s):
                copy.wait_send()

            @pl.when(inner)
            def _():
                outer = jnp.where(z < root, z - 1, z + 1)
                a_spread(s, 0, outer).wait_send()
                b_spread(s, 0, outer).wait_send()

        @pl.when(z == root)
        def _():
            yb_copy(s).wait_send()
            for way, to in ((0, z - 1), (1, z + 1)):
                a_spread(s, way, to).wait_send()
                b_spread(s, way, to).wait_send()

        @pl.when(owner)
        def _():
            src, dst = slab_a(s)
            for i, device in enumerate(others):
                remote(src, dst, sa_s.at[s, i], sa_r.at[s], device).wait_send()

        @pl.when(owner & in_slab(s))
        def _():
            src, dst = slab_b(s)
            for i, device in enumerate(others):
                remote(src, dst, sb_s.at[s, i], sb_r.at[s], device).wait_send()

        return carry

    lax.fori_loop(0, segments, drain, 0)
    for j in range(QUARTERS):
        out_copy(j).wait()


def gram_call(slices, basis):
    count, rows, depth = slices.shape
    rank = basis.shape[1]
    columns = rows // 2
    segments = count // 2 * QUARTERS
    roots = segments // 2
    a_rows = rows // (2 * QUARTERS)
    b_rows = rows // QUARTERS
    f32, bf16 = jnp.float32, jnp.bfloat16
    dma = pltpu.SemaphoreType.DMA
    scale = 1.0 / float(count * rank) ** 0.5
    return pl.pallas_call(
        functools.partial(gram_kernel, scale),
        out_shape=jax.ShapeDtypeStruct((rows, columns), f32),
        in_specs=[pl.BlockSpec(memory_space=pl.ANY), pl.BlockSpec(memory_space=pltpu.VMEM)],
        out_specs=pl.BlockSpec(memory_space=pl.ANY),
        scratch_shapes=[
            pltpu.VMEM((count, rows, rank), f32),
            pltpu.VMEM((count, rows, rank), f32),
            pltpu.VMEM((segments, a_rows, rank), f32),
            pltpu.VMEM((segments + roots, a_rows, rank), f32),
            pltpu.VMEM((segments + roots, b_rows, rank), f32),
            pltpu.VMEM((roots, b_rows, rank), f32),
            pltpu.VMEM((count, columns, rank), f32),
            pltpu.VMEM((2, 2 * a_rows + b_rows, depth), f32),
            pltpu.VMEM((depth, 2 * rank), bf16),
            pltpu.VMEM((6 * rank, columns), bf16),
            pltpu.VMEM((rows, columns), f32),
            dma((2, 3)),
            dma((segments,)), dma((segments,)),
            dma((segments,)), dma((segments + roots,)),
            dma((segments,)), dma((segments + roots,)),
            dma((roots,)), dma((roots,)),
            dma((segments, 2)), dma((segments,)),
            dma((segments, 2)), dma((segments,)),
            dma((segments,)), dma((segments,)),
            dma((segments, 3)), dma((segments,)),
            dma((segments, 3)), dma((segments,)),
            dma((QUARTERS,)),
        ],
        compiler_params=pltpu.CompilerParams(
            collective_id=0, has_side_effects=True, vmem_limit_bytes=62 * 2**20
        ),
        cost_estimate=pl.CostEstimate(
            flops=2 * count * rows * rank * (4 * depth + 3 * columns),
            bytes_accessed=4 * (count * rows * depth + rows * columns),
            transcendentals=0,
        ),
    )(slices, basis)


def from_root(block, axis, owner):
    block = jnp.where(lax.axis_index(axis) == owner, block, jnp.zeros_like(block))
    return lax.psum(block, axis)


def general(slices, basis):
    count = slices.shape[0]
    row_block = slices.shape[1]
    col_block = slices.shape[2]
    rank = basis.shape[1]
    partial_value = jnp.einsum(
        "kac,cr->kar",
        slices,
        basis,
        precision=lax.Precision.HIGHEST,
        preferred_element_type=jnp.float32,
    )
    projected = lax.psum(partial_value, "col")
    first_col = lax.axis_index("col") * col_block
    owner_row = first_col // row_block
    own_slab = lax.dynamic_slice_in_dim(projected, first_col % row_block, col_block, 1)
    column_slab = from_root(own_slab, "row", owner_row)
    scale = 1.0 / jnp.sqrt(jnp.float32(count * rank))
    outer = jnp.einsum(
        "kar,kbr->ab",
        projected,
        column_slab,
        precision=lax.Precision.HIGHEST,
        preferred_element_type=jnp.float32,
    )
    return outer * scale


def solution(mesh):
    placed = (P(None, "row", "col"), P("col", None))
    lined = mesh.shape["row"] == LINE and mesh.shape["col"] == 2 * LINE
    return jax.shard_map(
        gram_call if lined else general,
        mesh=mesh, in_specs=placed, out_specs=P("row", "col"), check_vma=False,
    )
```

```python
import functools

import jax
import jax.numpy as jnp
from jax import lax
from jax.experimental import pallas as pl
from jax.experimental.pallas import tpu as pltpu
from jax.sharding import PartitionSpec as P

MESH = pl.DeviceIdType.MESH
PIECES = 8
LINE = 4
LAG_END, LAG_INNER, LAG_ROOT, LAG_FINISH, LAG_SPREAD, LAG_OUTER, LAG_DONE = 2, 4, 6, 8, 10, 12, 14


def split(value):
    high = value.astype(jnp.bfloat16)
    low = (value - high.astype(jnp.float32)).astype(jnp.bfloat16)
    return high, low


def gram_kernel(
    scale, slices, basis, out,
    part, fin, y_in, za_in, zb_in, yb_in, slab, stream, factor, slab_t, acc,
    stream_sem, y_s, y_r, za_s, za_r, zb_s, zb_r, yb_s, yb_r,
    ca_s, ca_r, cb_s, cb_r, yg_s, yg_r, sa_s, sa_r, sb_s, sb_r, out_sem,
):
    count, rows, depth = slices.shape
    rank = basis.shape[1]
    pairs = count // 2
    segments = pairs * PIECES
    half = rows // 2
    a_rows = half // PIECES
    b_rows = rows // PIECES
    row = lax.axis_index("row")
    col = lax.axis_index("col")
    z, y = col // 2, col % 2
    mate = {"col": z * 2 + 1 - y}
    others = [{"row": lax.rem(row + i, 4)} for i in (1, 2, 3)]
    owner = row == z
    inner = (z > 0) & (z < LINE - 1)

    def at_z(position):
        return {"col": position * 2 + y}

    def place(s):
        return s // PIECES, s % PIECES

    def root_of(s):
        return LINE // 2 - 1 + s % 2

    def a_part(s, side):
        p, q = place(s)
        return p, pl.ds(pl.multiple_of(side * half + q * a_rows, a_rows), a_rows)

    def b_part(s):
        p, q = place(s)
        return pairs + p, pl.ds(pl.multiple_of(q * b_rows, b_rows), b_rows)

    def remote(src, dst, send, recv, device):
        return pltpu.make_async_remote_copy(
            src_ref=src, dst_ref=dst, send_sem=send, recv_sem=recv,
            device_id=device, device_id_type=MESH,
        )

    def stream_copies(s):
        slot = s % 2
        k, first = a_part(s, 0)
        _, second = a_part(s, 1)
        kb, all_b = b_part(s)
        return [
            pltpu.make_async_copy(slices.at[k, first], stream.at[slot, pl.ds(0, a_rows)], stream_sem.at[slot, 0]),
            pltpu.make_async_copy(slices.at[k, second], stream.at[slot, pl.ds(a_rows, a_rows)], stream_sem.at[slot, 1]),
            pltpu.make_async_copy(slices.at[kb, all_b], stream.at[slot, pl.ds(2 * a_rows, b_rows)], stream_sem.at[slot, 2]),
        ]

    def y_copy(s):
        k, there = a_part(s, 1 - y)
        return remote(part.at[k, there], y_in.at[s], y_s.at[s], y_r.at[s], mate)

    def z_copies(s):
        root = root_of(s)
        target = at_z(jnp.where(z < root, z + 1, jnp.maximum(z - 1, 0)))
        slot = jnp.where(z - 1 == root, segments + s // 2, s)
        k, mine = a_part(s, y)
        kb, all_b = b_part(s)
        return [
            remote(part.at[k, mine], za_in.at[slot], za_s.at[s], za_r.at[slot], target),
            remote(part.at[kb, all_b], zb_in.at[slot], zb_s.at[s], zb_r.at[slot], target),
        ]

    def yb_copy(s):
        kb, all_b = b_part(s)
        return remote(part.at[kb, all_b], yb_in.at[s // 2], yb_s.at[s // 2], yb_r.at[s // 2], mate)

    def a_spread(s, way, to):
        k, mine = a_part(s, y)
        return remote(fin.at[k, mine], fin.at[k, mine], ca_s.at[s, way], ca_r.at[s], at_z(to))

    def b_spread(s, way, to):
        kb, all_b = b_part(s)
        return remote(fin.at[kb, all_b], fin.at[kb, all_b], cb_s.at[s, way], cb_r.at[s], at_z(to))

    def y_gather(s, side):
        k, mine = a_part(s, side)
        return remote(fin.at[k, mine], fin.at[k, mine], yg_s.at[s], yg_r.at[s], mate)

    def slab_a(s):
        k, mine = a_part(s, y)
        _, q = place(s)
        return fin.at[k, mine], slab.at[k, pl.ds(pl.multiple_of(q * a_rows, a_rows), a_rows)]

    def slab_b(s):
        kb, all_b = b_part(s)
        _, q = place(s)
        return fin.at[kb, all_b], slab.at[kb, pl.ds(pl.multiple_of(q % (PIECES // 2) * b_rows, b_rows), b_rows)]

    def in_slab(s):
        return (s % PIECES) // (PIECES // 2) == y

    for copy in stream_copies(0):
        copy.start()

    high, low = split(basis[...])
    factor[:, :rank] = high
    factor[:, rank:] = low

    barrier = pltpu.get_barrier_semaphore()
    pl.semaphore_signal(barrier, inc=1, device_id=mate, device_id_type=MESH)
    for device in others:
        pl.semaphore_signal(barrier, inc=1, device_id=device, device_id_type=MESH)

    @pl.when(z > 0)
    def _():
        pl.semaphore_signal(barrier, inc=1, device_id=at_z(jnp.maximum(z - 1, 0)), device_id_type=MESH)

    @pl.when(z < LINE - 1)
    def _():
        pl.semaphore_signal(barrier, inc=1, device_id=at_z(jnp.minimum(z + 1, LINE - 1)), device_id_type=MESH)

    pl.semaphore_wait(barrier, jnp.where(inner, 6, 5))
    acc[...] = jnp.zeros_like(acc)

    def project(s):
        slot = s % 2

        @pl.when(s + 1 < segments)
        def _():
            for copy in stream_copies(s + 1):
                copy.start()

        for copy in stream_copies(s):
            copy.wait()
        p, q = place(s)
        for i in range(4):
            high, low = split(stream[slot, i * a_rows:(i + 1) * a_rows, :])
            both = jnp.dot(high, factor[...], preferred_element_type=jnp.float32)
            both += jnp.dot(low, factor[...], preferred_element_type=jnp.float32)
            value = both[:, :rank] + both[:, rank:]
            if i < 2:
                k, there = a_part(s, i)
            else:
                k = pairs + p
                there = pl.ds(pl.multiple_of(q * b_rows + (i - 2) * a_rows, a_rows), a_rows)
            part[k, there, :] = value
        y_copy(s).start()

    def arrive(buffer, slot, sem):
        pltpu.make_async_copy(buffer.at[slot], buffer.at[slot], sem.at[slot]).wait()

    def reduce_end(s):
        k, mine = a_part(s, y)

        @pl.when(jnp.logical_not(inner))
        def _():
            y_copy(s).wait_recv()
            part[k, mine, :] += y_in[s]
            for copy in z_copies(s):
                copy.start()

    def reduce_inner(s):
        k, mine = a_part(s, y)
        kb, all_b = b_part(s)

        @pl.when(inner & (z != root_of(s)))
        def _():
            y_copy(s).wait_recv()
            arrive(za_in, s, za_r)
            part[k, mine, :] += y_in[s] + za_in[s]
            arrive(zb_in, s, zb_r)
            part[kb, all_b, :] += zb_in[s]
            for copy in z_copies(s):
                copy.start()

    def reduce_root(s):
        k, mine = a_part(s, y)
        kb, all_b = b_part(s)
        second = segments + s // 2

        @pl.when(z == root_of(s))
        def _():
            y_copy(s).wait_recv()
            arrive(zb_in, s, zb_r)
            arrive(zb_in, second, zb_r)
            part[kb, all_b, :] += zb_in[s] + zb_in[second]
            yb_copy(s).start()
            arrive(za_in, s, za_r)
            arrive(za_in, second, za_r)
            fin[k, mine, :] = (part[k, mine, :] + y_in[s]) + (za_in[s] + za_in[second])
            a_spread(s, 0, z - 1).start()
            a_spread(s, 1, z + 1).start()
            y_gather(s, y).start()

    def finish_root(s):
        kb, all_b = b_part(s)

        @pl.when(z == root_of(s))
        def _():
            yb_copy(s).wait_recv()
            fin[kb, all_b, :] = part[kb, all_b, :] + yb_in[s // 2]
            b_spread(s, 0, z - 1).start()
            b_spread(s, 1, z + 1).start()

    def spread(s, here):
        root = root_of(s)
        outer = jnp.clip(jnp.where(z < root, z - 1, z + 1), 0, LINE - 1)

        @pl.when(here & (z != root))
        def _():
            a_spread(s, 0, outer).wait_recv()

            @pl.when(inner)
            def _():
                a_spread(s, 0, outer).start()

            y_gather(s, y).start()

        @pl.when(here & (z != root))
        def _():
            b_spread(s, 0, outer).wait_recv()

            @pl.when(inner)
            def _():
                b_spread(s, 0, outer).start()

        @pl.when(here & owner)
        def _():
            src, dst = slab_a(s)
            for i, device in enumerate(others):
                remote(src, dst, sa_s.at[s, i], sa_r.at[s], device).start()
            pltpu.make_async_copy(src, dst, sa_r.at[s]).start()

        @pl.when(here & owner & in_slab(s))
        def _():
            src, dst = slab_b(s)
            for i, device in enumerate(others):
                remote(src, dst, sb_s.at[s, i], sb_r.at[s], device).start()
            pltpu.make_async_copy(src, dst, sb_r.at[s]).start()

    def done(s):
        y_gather(s, 1 - y).wait_recv()
        src, dst = slab_a(s)
        pltpu.make_async_copy(src, dst, sa_r.at[s]).wait()

        @pl.when(in_slab(s))
        def _():
            src, dst = slab_b(s)
            pltpu.make_async_copy(src, dst, sb_r.at[s]).wait()

    def out_copy(j):
        here = pl.ds(pl.multiple_of(j * b_rows, b_rows), b_rows)
        return pltpu.make_async_copy(acc.at[here], out.at[here], out_sem.at[j])

    def multiply(s):
        p, j = place(s)

        @pl.when(j == 0)
        def _():
            for i, k in enumerate((p, pairs + p)):
                high, low = split((slab[k] * scale).T)
                slab_t[i * rank:(i + 1) * rank, :] = high
                slab_t[(2 + i) * rank:(3 + i) * rank, :] = high
                slab_t[(4 + i) * rank:(5 + i) * rank, :] = low

        for i in range(2):
            here = pl.ds(pl.multiple_of(j * b_rows + i * a_rows, a_rows), a_rows)
            high, low = split(jnp.concatenate([fin[p, here, :], fin[pairs + p, here, :]], axis=1))
            left = jnp.concatenate([high, low, high], axis=1)
            acc[here, :] += jnp.dot(left, slab_t[...], preferred_element_type=jnp.float32)

        @pl.when(p == pairs - 1)
        def _():
            out_copy(j).start()

    def stage(action, s):
        pl.when((s >= 0) & (s < segments))(lambda: action(s))

    def body(t, carry):
        stage(project, t)
        stage(reduce_end, t - LAG_END)
        stage(reduce_inner, t - LAG_INNER)
        stage(reduce_root, t - LAG_ROOT)
        stage(finish_root, t - LAG_FINISH)
        stage(lambda s: spread(s, inner), t - LAG_SPREAD)
        stage(lambda s: spread(s, jnp.logical_not(inner)), t - LAG_OUTER)
        stage(done, t - LAG_DONE)
        stage(multiply, t - LAG_DONE - PIECES + 1)
        return carry

    lax.fori_loop(0, segments + LAG_DONE + PIECES - 1, body, 0)

    def drain(s, carry):
        root = root_of(s)
        y_copy(s).wait_send()
        y_gather(s, y).wait_send()

        @pl.when(z != root)
        def _():
            for copy in z_copies(s):
                copy.wait_send()

            @pl.when(inner)
            def _():
                outer = jnp.where(z < root, z - 1, z + 1)
                a_spread(s, 0, outer).wait_send()
                b_spread(s, 0, outer).wait_send()

        @pl.when(z == root)
        def _():
            yb_copy(s).wait_send()
            for way, to in ((0, z - 1), (1, z + 1)):
                a_spread(s, way, to).wait_send()
                b_spread(s, way, to).wait_send()

        @pl.when(owner)
        def _():
            src, dst = slab_a(s)
            for i, device in enumerate(others):
                remote(src, dst, sa_s.at[s, i], sa_r.at[s], device).wait_send()

        @pl.when(owner & in_slab(s))
        def _():
            src, dst = slab_b(s)
            for i, device in enumerate(others):
                remote(src, dst, sb_s.at[s, i], sb_r.at[s], device).wait_send()

        return carry

    lax.fori_loop(0, segments, drain, 0)
    for j in range(PIECES):
        out_copy(j).wait()


def gram_call(slices, basis):
    count, rows, depth = slices.shape
    rank = basis.shape[1]
    columns = rows // 2
    segments = count // 2 * PIECES
    roots = segments // 2
    a_rows = rows // (2 * PIECES)
    b_rows = rows // PIECES
    f32, bf16 = jnp.float32, jnp.bfloat16
    dma = pltpu.SemaphoreType.DMA
    scale = 1.0 / float(count * rank) ** 0.5
    return pl.pallas_call(
        functools.partial(gram_kernel, scale),
        out_shape=jax.ShapeDtypeStruct((rows, columns), f32),
        in_specs=[pl.BlockSpec(memory_space=pl.ANY), pl.BlockSpec(memory_space=pltpu.VMEM)],
        out_specs=pl.BlockSpec(memory_space=pl.ANY),
        scratch_shapes=[
            pltpu.VMEM((count, rows, rank), f32),
            pltpu.VMEM((count, rows, rank), f32),
            pltpu.VMEM((segments, a_rows, rank), f32),
            pltpu.VMEM((segments + roots, a_rows, rank), f32),
            pltpu.VMEM((segments + roots, b_rows, rank), f32),
            pltpu.VMEM((roots, b_rows, rank), f32),
            pltpu.VMEM((count, columns, rank), f32),
            pltpu.VMEM((2, 2 * a_rows + b_rows, depth), f32),
            pltpu.VMEM((depth, 2 * rank), bf16),
            pltpu.VMEM((6 * rank, columns), bf16),
            pltpu.VMEM((rows, columns), f32),
            dma((2, 3)),
            dma((segments,)), dma((segments,)),
            dma((segments,)), dma((segments + roots,)),
            dma((segments,)), dma((segments + roots,)),
            dma((roots,)), dma((roots,)),
            dma((segments, 2)), dma((segments,)),
            dma((segments, 2)), dma((segments,)),
            dma((segments,)), dma((segments,)),
            dma((segments, 3)), dma((segments,)),
            dma((segments, 3)), dma((segments,)),
            dma((PIECES,)),
        ],
        compiler_params=pltpu.CompilerParams(
            collective_id=0, has_side_effects=True, vmem_limit_bytes=62 * 2**20
        ),
        cost_estimate=pl.CostEstimate(
            flops=2 * count * rows * rank * (4 * depth + 3 * columns),
            bytes_accessed=4 * (count * rows * depth + rows * columns),
            transcendentals=0,
        ),
    )(slices, basis)


def from_root(block, axis, owner):
    block = jnp.where(lax.axis_index(axis) == owner, block, jnp.zeros_like(block))
    return lax.psum(block, axis)


def general(slices, basis):
    count = slices.shape[0]
    row_block = slices.shape[1]
    col_block = slices.shape[2]
    rank = basis.shape[1]
    partial_value = jnp.einsum(
        "kac,cr->kar",
        slices,
        basis,
        precision=lax.Precision.HIGHEST,
        preferred_element_type=jnp.float32,
    )
    projected = lax.psum(partial_value, "col")
    first_col = lax.axis_index("col") * col_block
    owner_row = first_col // row_block
    own_slab = lax.dynamic_slice_in_dim(projected, first_col % row_block, col_block, 1)
    column_slab = from_root(own_slab, "row", owner_row)
    scale = 1.0 / jnp.sqrt(jnp.float32(count * rank))
    outer = jnp.einsum(
        "kar,kbr->ab",
        projected,
        column_slab,
        precision=lax.Precision.HIGHEST,
        preferred_element_type=jnp.float32,
    )
    return outer * scale


def solution(mesh):
    placed = (P(None, "row", "col"), P("col", None))
    lined = mesh.shape["row"] == LINE and mesh.shape["col"] == 2 * LINE
    return jax.shard_map(
        gram_call if lined else general,
        mesh=mesh, in_specs=placed, out_specs=P("row", "col"), check_vma=False,
    )
```
